256 devices in a mesh: prow: 8 (over x, core), pcol: 32 (over z, y).
Axes of the slice: x: 4, y: 4, z: 8, core: 2. Of those that a mesh axis runs over, the one named last changes fastest.
Arguments:
- kernel: float32 [8, 8, 256, 2, 32, 256], P(None, 'prow', None, None, 'pcol'), as said below
Outputs:
- factored: float32 [8, 8, 256, 2, 32, 256], P(None, 'prow', None, None, 'pcol')
Inputs may be any that keep to these rules, and one draw needn't show every extreme that they name: kernel read as a matrix is a symmetric positive definite covariance matrix.
All inputs are finite; a program needn't handle non-finite values.
Results may differ from the reference program's by a relative error of at most 0.0003.
Values sent between devices are 32-bit elements; how exact they have to be, the bound alone decides.
No kernel may reach another device: no remote copies, remote signals or barrier semaphores. Data moves between devices by JAX's collectives and lax.ppermute only.
A program may use at most 64 MiB of HBM per device.

```python
import jax
import jax.numpy as jnp
from jax import lax

N = 16384
NB = 256
STEPS = 2
LR = 8
LC = 2


def draw_kernel(key, part):
    key = jax.random.fold_in(key, 1)
    key_points, key_nugget, key_scale = jax.random.split(key, 3)
    points = jax.random.normal(key_points, (8, N), jnp.float32)
    scales = jnp.exp(jax.random.uniform(key_scale, (N,), jnp.float32, 0.0, 0.7))
    separation = jnp.zeros((N, N), jnp.float32)
    for component in range(8):
        across = points[component][:, None] - points[component][None, :]
        separation = separation + across * across
    nugget = jax.random.uniform(key_nugget, (N,), jnp.float32, 0.3, 0.6)
    positions = jnp.arange(N)
    matrix = jnp.exp(separation * -0.125)
    matrix = matrix + jnp.where(positions[:, None] == positions[None, :], nugget[:, None], 0.0)
    matrix = scales[:, None] * matrix * scales[None, :]
    return matrix.reshape(LR, N // (LR * NB), NB, LC, N // (LC * NB), NB)


def setup_inputs(seed: int = 0) -> dict:
    seeds = jax.random.split(jax.random.key(seed), 2)
    kernel = draw_kernel(jax.random.fold_in(seeds[1], 71), 0)
    return {"kernel": kernel}


def reference(kernel):
    matrix = kernel.reshape(N, N)
    identity = jnp.eye(NB, dtype=jnp.float32)
    for section in range(STEPS):
        low, high = (section * NB, (section + 1) * NB)
        factor = jnp.linalg.cholesky(matrix[low:high, low:high])
        inverse = jax.scipy.linalg.solve_triangular(factor, identity, lower=True)
        below = jnp.dot(matrix[high:, low:high], inverse.T, precision=lax.Precision.HIGHEST)
        trailing = matrix[high:, high:] - jnp.dot(below, below.T, precision=lax.Precision.HIGHEST)
        matrix = matrix.at[high:, high:].set(trailing)
        matrix = matrix.at[low:high, high:].set(0.0)
        matrix = matrix.at[low:high, low:high].set(factor)
        matrix = matrix.at[high:, low:high].set(below)
    return matrix.reshape(kernel.shape)
```

```python
import jax
import jax.numpy as jnp
from jax import lax
from jax.experimental import pallas as pl
from jax.experimental.pallas import tpu as pltpu
from jax.sharding import PartitionSpec as P

AXES = ("prow", "pcol")
ROWS, COLS = 8, 32
HIGHEST = lax.Precision.HIGHEST


def dot(a, b, dims=((1,), (0,))):
    return lax.dot_general(
        a, b, (dims, ((), ())), precision=HIGHEST, preferred_element_type=jnp.float32
    )


def send(value, pairs):
    flat = [(p * COLS + s, u * COLS + v) for (p, s), (u, v) in pairs]
    return lax.ppermute(value, AXES, flat)


def swap_cores(value):
    return send(value, [((p, s), (p ^ 1, s)) for p in range(ROWS) for s in range(COLS)])


def along_x(value, cols):
    parts = [
        send(value, [((p, s), (2 * k + p, s)) for p in range(2) for s in cols]) for k in (1, 2, 3)
    ]
    return value + (parts[0] + parts[1] + parts[2])


def along_y(value):
    parts = [send(value, [((p, 0), (p, k)) for p in range(ROWS)]) for k in (1, 2, 3)]
    return value + (parts[0] + parts[1] + parts[2])


def along_z(value):
    parts = [
        send(value, [((p, y), (p, 4 * k + y)) for p in range(ROWS) for y in range(4)])
        for k in range(1, 8)
    ]
    total = value
    for part in parts:
        total = total + part
    return total


def scatter_rows(own):
    parts = []
    for i in range(8):
        pairs = []
        for q in range(4):
            for t in range(8):
                s = 8 * q + t
                pairs.append(((0, s), (t, 8 * q + i)))
                pairs.append(((1, s), (t, 8 * q + (i + 4) % 8)))
        parts.append(send(own[128 * i : 128 * (i + 1)], pairs))
    low = (parts[0] + parts[1]) + (parts[2] + parts[3])
    high = (parts[4] + parts[5]) + (parts[6] + parts[7])
    return jnp.concatenate([low, high], axis=0)


def eliminate(block):
    sub = lax.broadcasted_iota(jnp.int32, (8, 128), 0)
    lane = lax.broadcasted_iota(jnp.int32, (8, 128), 1)
    left, right = [], []
    for i in range(16):
        left.append(block[8 * i : 8 * i + 8, :])
        right.append(jnp.where(lane == sub + 8 * i, 1.0, 0.0))
    for b in range(16):
        for j in range(8):
            c = 8 * b + j
            row_left, row_right = left[b][j : j + 1, :], right[b][j : j + 1, :]
            scale = 1.0 / row_left[:, c : c + 1]
            row_left, row_right = row_left * scale, row_right * scale
            for i in range(b, 16):
                if i == b and j == 7:
                    continue
                column = left[i][:, c : c + 1]
                if i == b:
                    column = jnp.where(sub[:, :1] > j, column, 0.0)
                left[i] = left[i] - column * row_left
                right[i] = right[i] - column * row_right
    upper, inverse = [], []
    for i in range(16):
        pivot = jnp.sum(jnp.where(lane == sub + 8 * i, left[i], 0.0), axis=1, keepdims=True)
        scale = lax.rsqrt(pivot)
        upper.append(jnp.where(lane >= sub + 8 * i, left[i] * scale, 0.0))
        inverse.append(right[i] * scale)
    return jnp.concatenate(upper, 0), jnp.concatenate(inverse, 0)


def factor_kernel(place, first, first_other, second, second_other, upper, inverse, work):
    odd = place[0] % 2 == 1
    for h in range(2):
        lanes = slice(128 * h, 128 * h + 128)
        far = slice(256 + 128 * h, 384 + 128 * h)
        mine = first[pl.ds(h, 128, stride=2), :]
        other = first_other[pl.ds(h, 128, stride=2), :]
        work[0:128, lanes] = jnp.where(odd, other, mine)
        work[128:256, lanes] = jnp.where(odd, mine, other)
        mine = second[pl.ds(h, 256, stride=2), :]
        other = second_other[pl.ds(h, 256, stride=2), :]
        work[0:256, far] = jnp.where(odd, other, mine)
        work[256:512, far] = jnp.where(odd, mine, other)
    work[256:512, 0:256] = jnp.zeros((256, 256), jnp.float32)
    row = lax.broadcasted_iota(jnp.int32, (512, 512), 0)
    col = lax.broadcasted_iota(jnp.int32, (512, 512), 1)
    work[:, 512:] = jnp.where(row == col, 1.0, 0.0)
    upper[...] = jnp.zeros((512, 512), jnp.float32)
    inverse[...] = jnp.zeros((512, 512), jnp.float32)
    for k in range(4):
        lo, hi = 128 * k, 128 * k + 128
        up, inv = eliminate(work[lo:hi, lo:hi])
        upper[lo:hi, lo:hi] = up
        inverse[lo:hi, lo:hi] = inv
        if k:
            inverse[lo:hi, :lo] = dot(inv, work[lo:hi, 512 : 512 + lo])
        if k < 3:
            right = dot(inv, work[lo:hi, hi:512])
            upper[lo:hi, hi:] = right
            work[hi:512, hi:512] -= dot(right, right, ((0,), (0,)))
            work[hi:512, 512 : 512 + hi] -= dot(right, inverse[lo:hi, :hi], ((0,), (0,)))


def factor(place, first, first_other, second, second_other):
    square = jax.ShapeDtypeStruct((512, 512), jnp.float32)
    vmem = pl.BlockSpec(memory_space=pltpu.VMEM)
    return pl.pallas_call(
        factor_kernel,
        out_shape=(square, square),
        in_specs=[pl.BlockSpec(memory_space=pltpu.SMEM)] + [vmem] * 4,
        out_specs=(vmem, vmem),
        scratch_shapes=[pltpu.VMEM((512, 1024), jnp.float32)],
        compiler_params=pltpu.CompilerParams(vmem_limit_bytes=32 << 20),
        cost_estimate=pl.CostEstimate(flops=40_000_000_000, bytes_accessed=4 << 20, transcendentals=0),
        name="factor",
    )(place, first, first_other, second, second_other)


def update_kernel(place, a, gathered, mine, other, upper, inverse, out, weight, lhs):
    r = pl.program_id(0)
    p, s = place[0], place[1]

    @pl.when(r == 0)
    def _():
        odd = p % 2 == 1
        for ch in range(4):
            lanes = slice(128 * ch, 128 * ch + 128)
            here, there = mine[pl.ds(ch, 256, stride=4), :], other[pl.ds(ch, 256, stride=4), :]
            weight[0:256, lanes] = jnp.where(odd, there, here)
            weight[256:512, lanes] = jnp.where(odd, here, there)
        half = dot(inverse[...], weight[...])
        row = lax.broadcasted_iota(jnp.int32, (512, 512), 0)
        col = lax.broadcasted_iota(jnp.int32, (512, 512), 1)
        pick = jnp.where(row == col + 256 * s, -1.0, 0.0)
        half = jnp.where((col < 256) & (s < 2), pick, half)
        weight[...] = dot(inverse[...], half, ((0,), (0,)))

    c, q = r // 4, r % 4
    for t in range(8):
        for slot in range(2):
            if t < 4:
                k = 32 * t if slot == 0 else 256 + 32 * (t + 4)
            else:
                k = 256 + 32 * (t - 4) if slot == 0 else 32 * t
            for h in range(2):
                start = q * 2048 + (t * 256 + slot * 128 + h) + 2 * c
                lhs[k : k + 32, 128 * h : 128 * h + 128] = gathered[pl.ds(start, 32, stride=4), :]
    product = dot(lhs[...], weight[...], ((0,), (0,)))
    for ch in range(4):
        kept = a[pl.ds(ch, 256, stride=4), :]
        if ch < 2:
            kept = jnp.where(s < 2, 0.0, kept)
        out[pl.ds(ch, 256, stride=4), :] = kept - product[:, 128 * ch : 128 * ch + 128]

    @pl.when((r == 0) & (p < 2))
    def _():
        for ch in range(4):
            where = pl.ds(ch, 256, stride=4)
            if ch >= 2:
                out[where, :] = jnp.zeros((256, 128), jnp.float32)
            else:
                lanes = slice(128 * ch, 128 * ch + 128)
                near = jnp.where(p == 0, upper[lanes, 0:256], upper[256 + 128 * ch : 384 + 128 * ch, 256:512])
                diagonal = near.T
                natural = out[where, :]
                out[where, :] = jnp.where(s == p, diagonal, jnp.where(s > p, 0.0, natural))


def update(place, a, gathered, mine, other, upper, inverse):
    vmem = pl.BlockSpec(memory_space=pltpu.VMEM)
    return pl.pallas_call(
        update_kernel,
        out_shape=jax.ShapeDtypeStruct(a.shape, jnp.float32),
        grid=(8,),
        in_specs=[
            pl.BlockSpec(memory_space=pltpu.SMEM),
            pl.BlockSpec((1024, 128), lambda r: (r, 0)),
            vmem,
            vmem,
            vmem,
            vmem,
            vmem,
        ],
        out_specs=pl.BlockSpec((1024, 128), lambda r: (r, 0)),
        scratch_shapes=[
            pltpu.VMEM((512, 512), jnp.float32),
            pltpu.VMEM((512, 256), jnp.float32),
        ],
        compiler_params=pltpu.CompilerParams(vmem_limit_bytes=40 << 20),
        cost_estimate=pl.CostEstimate(flops=8_000_000_000, bytes_accessed=16 << 20, transcendentals=0),
        name="update",
    )(place, a, gathered, mine, other, upper, inverse)


def per_device(kernel):
    p, s = lax.axis_index("prow"), lax.axis_index("pcol")
    place = jnp.stack([p, s]).astype(jnp.int32)
    a = kernel.reshape(8192, 128)
    own = a[:1024]

    gathered = lax.all_gather(scatter_rows(own), "pcol", tiled=True)

    block = own.reshape(256, 4, 128)[:, :2].reshape(512, 128)
    root = (p == 0) & (s == 0)
    first = send(block[256:], [((0, 0), (1, 0))])
    first = jnp.where(root, block[:256], first)
    first = along_z(along_y(along_x(first, (0,))))
    second = send(block, [((0, 1), (0, 0)), ((1, 1), (1, 0))])
    second = along_z(along_y(along_x(second, (0,))))
    upper, inverse = factor(place, first, swap_cores(first), second, swap_cores(second))

    mine = along_x(jnp.where(p < 2, own, 0.0), range(COLS))
    other = swap_cores(mine)
    out = update(place, a, gathered, mine, other, upper, inverse)
    return out.reshape(kernel.shape)


def solution(mesh):
    spec = P(None, "prow", None, None, "pcol", None)
    return jax.shard_map(per_device, mesh=mesh, in_specs=(spec,), out_specs=spec, check_vma=False)
```

```python
import jax
import jax.numpy as jnp
from jax import lax
from jax.experimental import pallas as pl
from jax.experimental.pallas import tpu as pltpu
from jax.sharding import PartitionSpec as P

AXES = ("prow", "pcol")
ROWS, COLS = 8, 32
HIGHEST = lax.Precision.HIGHEST


def dot(a, b, dims=((1,), (0,))):
    return lax.dot_general(
        a, b, (dims, ((), ())), precision=HIGHEST, preferred_element_type=jnp.float32
    )


def send(value, pairs):
    flat = [(p * COLS + s, u * COLS + v) for (p, s), (u, v) in pairs]
    return lax.ppermute(value, AXES, flat)


def swap_cores(value):
    return send(value, [((p, s), (p ^ 1, s)) for p in range(ROWS) for s in range(COLS)])


def shifted(value, dx=0, dy=0, dz=0, keep=lambda p, s: True):
    pairs = []
    for p in range(ROWS):
        for s in range(COLS):
            if keep(p, s):
                z, y = divmod(s, 4)
                pairs.append(
                    ((p, s), ((p + 2 * dx) % ROWS, (z + dz) % 8 * 4 + (y + dy) % 4))
                )
    return send(value, pairs)


def after(value, *others):
    return lax.optimization_barrier((value, *others))[0]


def together(*values):
    return lax.optimization_barrier(values)


def stage(value, index, cores=(0, 1), root_y=0):
    moves, at_x, at_y, at_z = (
        ([{"dy": 1}, {"dy": 3}, {"dy": 2}], (0,), (root_y,), (0,)),
        ([{"dz": 3}, {"dz": 5}], (0,), (0, 1, 2, 3), (0,)),
        ([{"dz": 1}, {"dz": 7}], (0,), (0, 1, 2, 3), (0, 3, 5)),
        ([{"dx": 1}, {"dx": 3}, {"dx": 2}], (0,), (0, 1, 2, 3), range(8)),
    )[index]
    parts = []
    for move in moves:
        zs = (0, 3) if move == {"dz": 7} else at_z

        def keep(p, s, zs=zs):
            return p // 2 in at_x and p % 2 in cores and s % 4 in at_y and s // 4 in zs

        parts.append(shifted(value, keep=keep, **move))
    return parts


def scatter_rows(own):
    parts = []
    for i in range(4):
        pairs = []
        for q in range(4):
            for t in range(8):
                row = 8 * q + t // 4 * 4
                pairs.append(((0, 8 * q + t), (t, row + i)))
                pairs.append(((1, 8 * q + t), (t, row + (i + 2) % 4)))
        parts.append(send(own[256 * i : 256 * (i + 1)], pairs))
    return parts


def halve_rows(parts):
    low, high = parts[0] + parts[1], parts[2] + parts[3]
    here = jnp.concatenate([low[:128], high[:128]], axis=0)
    there = jnp.concatenate([low[128:], high[128:]], axis=0)
    pairs = []
    for q in range(ROWS):
        for c in range(0, COLS, 8):
            for y in range(4):
                z = q // 4 * 4
                pairs.append(((q, c + z + y), (q, c + 4 - z + y)))
    return here, send(there, pairs)


def eliminate(block):
    sub = lax.broadcasted_iota(jnp.int32, (8, 128), 0)
    lane = lax.broadcasted_iota(jnp.int32, (8, 128), 1)
    full = lambda x: jnp.broadcast_to(x, (8, 128))
    left = [block[8 * i : 8 * i + 8, :] for i in range(16)]
    right = [jnp.where(lane == sub + 8 * i, 1.0, 0.0) for i in range(16)]
    upper, inverse = [], []
    for b in range(16):
        c = 8 * b
        rows = left[b]
        cols = [full(rows[:, c + k : c + k + 1]) for k in range(8)]
        e = [[full(cols[k][i : i + 1, :]) if i >= k else None for k in range(8)] for i in range(8)]
        rec = []
        low = [[None] * 8 for _ in range(8)]
        for j in range(8):
            rec.append(1.0 / e[j][j])
            for i in range(j + 1, 8):
                low[i][j] = e[i][j] * rec[j]
            for i in range(j + 1, 8):
                for k in range(j + 1, i + 1):
                    e[i][k] = e[i][k] - low[i][j] * e[k][j]
        n = [[None] * 8 for _ in range(8)]
        for j in range(8):
            for i in range(j + 1, 8):
                t = low[i][j]
                for k in range(j + 1, i):
                    t = t + low[i][k] * n[k][j]
                n[i][j] = -t
        scale = [lax.rsqrt(e[j][j]) for j in range(8)]
        s = [[None] * 8 for _ in range(8)]
        for i in range(8):
            for j in range(i + 1):
                t = rec[i] * n[i][j] if j < i else rec[i]
                for k in range(i + 1, 8):
                    t = t + (n[k][i] * rec[k]) * n[k][j]
                s[i][j] = t
                s[j][i] = t
        row_left = [full(rows[k : k + 1, :]) for k in range(8)]
        row_right = [full(right[b][k : k + 1, :]) for k in range(8)]
        def stack(parts):
            v = parts[0]
            for i in range(1, 8):
                if parts[i] is not None:
                    v = jnp.where(sub == i, parts[i], v if v is not None else 0.0)
            return v if v is not None else None
        gl = gr = ul = ur = None
        for k in range(8):
            sc = stack([s[i][k] for i in range(8)])
            col = jnp.where(sub == k, scale[k], 0.0)
            for i in range(k + 1, 8):
                col = jnp.where(sub == i, n[i][k] * scale[i], col)
            a1, a2, a3, a4 = sc * row_left[k], sc * row_right[k], col * row_left[k], col * row_right[k]
            gl = a1 if gl is None else gl + a1
            gr = a2 if gr is None else gr + a2
            ul = a3 if ul is None else ul + a3
            ur = a4 if ur is None else ur + a4
        upper.append(jnp.where(lane >= sub + c, ul, 0.0))
        inverse.append(ur)
        gl_rows = [full(gl[k : k + 1, :]) for k in range(8)]
        gr_rows = [full(gr[k : k + 1, :]) for k in range(8)]
        for i in range(b + 1, 16):
            tl = tr = None
            for k in range(8):
                f = full(left[i][:, c + k : c + k + 1])
                x, y = f * gl_rows[k], f * gr_rows[k]
                tl = x if tl is None else tl + x
                tr = y if tr is None else tr + y
            left[i] = left[i] - tl
            right[i] = right[i] - tr
    return jnp.concatenate(upper, 0), jnp.concatenate(inverse, 0)


def factor_part(work, upper, inverse):
    upper[128:256, 0:128] = jnp.zeros((128, 128), jnp.float32)
    inverse[0:128, 128:256] = jnp.zeros((128, 128), jnp.float32)

    @pl.loop(0, 2)
    def _(k):
        here = pl.ds(pl.multiple_of(128 * k, 128), 128)
        up, inv = eliminate(work[here, here])
        upper[here, here] = up
        inverse[here, here] = inv

        @pl.when(k == 0)
        def _():
            right = dot(inv, work[0:128, 128:256])
            upper[0:128, 128:256] = right
            work[128:256, 128:256] -= dot(right, right, ((0,), (0,)))

    down = dot(upper[0:128, 128:256], inverse[0:128, 0:128], ((0,), (0,)))
    inverse[128:256, 0:128] = -dot(inverse[128:256, 128:256], down)


def factor_first_kernel(mine, other, upper, inverse, work):
    for h in range(2):
        rows = pl.ds(h, 128, stride=2)
        work[0:128, 128 * h : 128 * h + 128] = mine[rows, :] + other[rows, :]
    work[128:256, 128:256] = mine[256:384, :] + other[256:384, :]
    factor_part(work, upper, inverse)


def factor_second_kernel(place, mine, other, upper0, inverse0, upper, inverse, work, up, inv):
    odd = place[0] % 2 == 1
    side = up
    for h in range(2):
        lanes = slice(128 * h, 128 * h + 128)
        here, there = mine[pl.ds(h, 256, stride=2), :], other[pl.ds(h, 256, stride=2), :]
        side[:, lanes] = jnp.where(odd, there, here)
        work[:, lanes] = jnp.where(odd, here, there)
    right = dot(inverse0[...], side[...])
    work[...] -= dot(right, right, ((0,), (0,)))
    factor_part(work, up, inv)
    zero = jnp.zeros((256, 256), jnp.float32)
    upper[0] = upper0[...]
    upper[1] = up[...]
    inverse[0:256, 0:256] = inverse0[...]
    inverse[0:256, 256:512] = zero
    inverse[256:512, 256:512] = inv[...]
    inverse[256:512, 0:256] = -dot(inv[...], dot(right, inverse0[...], ((0,), (0,))))


VMEM = pl.BlockSpec(memory_space=pltpu.VMEM)
SMEM = pl.BlockSpec(memory_space=pltpu.SMEM)


def factor_first(mine, other):
    block = jax.ShapeDtypeStruct((256, 256), jnp.float32)
    return pl.pallas_call(
        factor_first_kernel,
        out_shape=(block, block),
        in_specs=[VMEM, VMEM],
        out_specs=(VMEM, VMEM),
        scratch_shapes=[pltpu.VMEM((256, 256), jnp.float32)],
        compiler_params=pltpu.CompilerParams(vmem_limit_bytes=16 << 20),
        cost_estimate=pl.CostEstimate(flops=60_000_000_000, bytes_accessed=1 << 20, transcendentals=0),
        name="factor_first",
    )(mine, other)


def factor_second(place, mine, other, upper, inverse):
    return pl.pallas_call(
        factor_second_kernel,
        out_shape=(
            jax.ShapeDtypeStruct((2, 256, 256), jnp.float32),
            jax.ShapeDtypeStruct((512, 512), jnp.float32),
        ),
        in_specs=[SMEM, VMEM, VMEM, VMEM, VMEM],
        out_specs=(VMEM, VMEM),
        scratch_shapes=[pltpu.VMEM((256, 256), jnp.float32) for _ in range(3)],
        compiler_params=pltpu.CompilerParams(vmem_limit_bytes=16 << 20),
        cost_estimate=pl.CostEstimate(flops=60_000_000_000, bytes_accessed=1 << 20, transcendentals=0),
        name="factor_second",
    )(place, mine, other, upper, inverse)


FAR_Z = (0, 1, 7, 2, 6, 3, 5, 4)
FAR_Y = (0, 1, 3, 2)


def split(value):
    high = value.astype(jnp.bfloat16)
    return high, (value - high.astype(jnp.float32)).astype(jnp.bfloat16)


def update_kernel(place, a, *refs):
    parts, (mine, other, upper, inverse, out, weight, high, low, w_high, w_low) = refs[:9], refs[9:]
    r = pl.program_id(0)
    p, s = place[0], place[1]

    @pl.when(r == 0)
    def _():
        for g in range(8):
            zz = (s // 4 + 8 - FAR_Z[g]) % 8
            q, late = zz // 2, jnp.where(zz % 2 == p // 4, 0, 32)
            for u in range(4):
                yy = (s % 4 + 4 - FAR_Y[u]) % 4
                part, first = (parts[g], 256 * u) if g < 7 else (parts[7 + u // 2], 256 * (u % 2))
                for slot in range(2):
                    if slot == 0:
                        k = jnp.where(yy < 2, 64 * yy, 128 + 64 * yy) + late
                    else:
                        k = jnp.where(yy < 2, 384 + 64 * yy, 64 * yy) + late
                    rows = pl.ds(pl.multiple_of(q * 512 + k, 32), 32)
                    for ch in range(4):
                        lanes = slice(128 * ch, 128 * ch + 128)
                        value = part[pl.ds(first + 128 * slot + ch, 32, stride=4), :]
                        high[rows, lanes], low[rows, lanes] = split(value)
        odd = p % 2 == 1
        for ch in range(4):
            lanes = slice(128 * ch, 128 * ch + 128)
            here, there = mine[pl.ds(ch, 256, stride=4), :], other[pl.ds(ch, 256, stride=4), :]
            weight[0:256, lanes] = jnp.where(odd, there, here)
            weight[256:512, lanes] = jnp.where(odd, here, there)
        half = dot(inverse[...], weight[...])
        row = lax.broadcasted_iota(jnp.int32, (512, 512), 0)
        col = lax.broadcasted_iota(jnp.int32, (512, 512), 1)
        pick = jnp.where(row == col + 256 * s, -1.0, 0.0)
        half = jnp.where((col < 256) & (s < 2), pick, half)
        w_high[...], w_low[...] = split(dot(inverse[...], half, ((0,), (0,))))

    c, q = r // 4, r % 4
    block = (pl.ds(pl.multiple_of(q * 512, 512), 512), pl.ds(pl.multiple_of(c * 256, 256), 256))
    x_high, x_low = high[block], low[block]

    def times(x, w):
        return lax.dot_general(x, w, (((0,), (0,)), ((), ())), preferred_element_type=jnp.float32)

    product = times(x_high, w_high[...]) + (times(x_high, w_low[...]) + times(x_low, w_high[...]))
    for ch in range(4):
        kept = a[pl.ds(ch, 256, stride=4), :]
        if ch < 2:
            kept = jnp.where(s < 2, 0.0, kept)
        out[pl.ds(ch, 256, stride=4), :] = kept - product[:, 128 * ch : 128 * ch + 128]

    @pl.when((r == 0) & (p < 2))
    def _():
        for ch in range(4):
            where = pl.ds(ch, 256, stride=4)
            if ch >= 2:
                out[where, :] = jnp.zeros((256, 128), jnp.float32)
            else:
                diagonal = upper[jnp.minimum(p, 1), 128 * ch : 128 * ch + 128, :].T
                natural = out[where, :]
                out[where, :] = jnp.where(s == p, diagonal, jnp.where(s > p, 0.0, natural))


def update(place, a, parts, mine, other, upper, inverse):
    return pl.pallas_call(
        update_kernel,
        out_shape=jax.ShapeDtypeStruct(a.shape, jnp.float32),
        grid=(8,),
        in_specs=[SMEM, pl.BlockSpec((1024, 128), lambda r: (r, 0))] + [VMEM] * 13,
        out_specs=pl.BlockSpec((1024, 128), lambda r: (r, 0)),
        scratch_shapes=[
            pltpu.VMEM((512, 512), jnp.float32),
            pltpu.VMEM((2048, 512), jnp.bfloat16),
            pltpu.VMEM((2048, 512), jnp.bfloat16),
            pltpu.VMEM((512, 512), jnp.bfloat16),
            pltpu.VMEM((512, 512), jnp.bfloat16),
        ],
        compiler_params=pltpu.CompilerParams(vmem_limit_bytes=40 << 20),
        cost_estimate=pl.CostEstimate(flops=8_000_000_000, bytes_accessed=16 << 20, transcendentals=0),
        name="update",
    )(place, a, *parts, mine, other, upper, inverse)


def per_device(kernel):
    p, s = lax.axis_index("prow"), lax.axis_index("pcol")
    place = jnp.stack([p, s]).astype(jnp.int32)
    a = kernel.reshape(8192, 128)
    own = a[:1024]
    block = own.reshape(256, 4, 128)[:, :2]

    rows = scatter_rows(own)

    first = jnp.concatenate([block[:128].reshape(256, 128), block[128:, 1]], axis=0)
    first = jnp.where((p == 0) & (s == 0), first, sum(stage(first, 0, (0,))))
    second = together(block.reshape(512, 128), first)[0]
    second = jnp.where((p < 2) & (s == 1), second, sum(stage(second, 0, (0, 1), 1)))
    first = first + sum(stage(first, 1, (0,)))
    first = first + sum(stage(first, 2, (0,)))
    here, moved = halve_rows(rows)
    near = jnp.where(p // 4 == s // 4 % 2, here, moved)
    near = together(near, first)[0]
    column = [near] + [shifted(near, dy=k) for k in (1, 3, 2)]
    column = jnp.concatenate(column, axis=0)
    second = second + sum(stage(second, 1))
    parts = stage(first, 3, (0,))
    column, second, first = together(column, second, first)

    up1, down1 = shifted(column, dz=1), shifted(column, dz=7)
    first = first + sum(parts)
    first_other = send(first, [((q, c), (q + 1, c)) for q in range(0, ROWS, 2) for c in range(COLS)])
    parts = stage(second, 2)
    up1, down1, first, first_other, second, *parts = together(
        up1, down1, first, first_other, second, *parts
    )

    second = second + sum(parts)
    parts = stage(second, 3)
    up2, down2 = shifted(up1, dz=1), shifted(down1, dz=7)
    upper, inverse = factor_first(first, first_other)
    up2, down2, second, upper, inverse, *parts = together(
        up2, down2, second, upper, inverse, *parts
    )

    second = second + sum(parts)
    second_other = swap_cores(second)
    mine = stage(together(own, upper)[0], 3)
    up3, down3 = shifted(up2, dz=1), shifted(down2, dz=7)
    upper, inverse = factor_second(place, second, second_other, upper, inverse)
    up3, down3, upper, inverse = together(up3, down3, upper, inverse)

    up4, down4 = shifted(up3[:512], dz=1), shifted(down3[512:], dz=7)
    up4, down4, *mine = together(up4, down4, *mine)
    mine = jnp.where(p < 2, own, sum(mine))
    other = swap_cores(mine)
    parts = [column, up1, down1, up2, down2, up3, down3, up4, down4]
    out = update(place, a, parts, mine, other, upper, inverse)
    return out.reshape(kernel.shape)


def solution(mesh):
    spec = P(None, "prow", None, None, "pcol", None)
    return jax.shard_map(per_device, mesh=mesh, in_specs=(spec,), out_specs=spec, check_vma=False)
```

```python
import jax
import jax.numpy as jnp
from jax import lax
from jax.experimental import pallas as pl
from jax.experimental.pallas import tpu as pltpu
from jax.sharding import PartitionSpec as P

AXES = ("prow", "pcol")
ROWS, COLS = 8, 32
HIGHEST = lax.Precision.HIGHEST


def dot(a, b, dims=((1,), (0,))):
    return lax.dot_general(
        a, b, (dims, ((), ())), precision=HIGHEST, preferred_element_type=jnp.float32
    )


def send(value, pairs):
    flat = [(p * COLS + s, u * COLS + v) for (p, s), (u, v) in pairs]
    return lax.ppermute(value, AXES, flat)


def swap_cores(value):
    return send(value, [((p, s), (p ^ 1, s)) for p in range(ROWS) for s in range(COLS)])


def shifted(value, dx=0, dy=0, dz=0, keep=lambda p, s: True):
    pairs = []
    for p in range(ROWS):
        for s in range(COLS):
            if keep(p, s):
                z, y = divmod(s, 4)
                pairs.append(
                    ((p, s), ((p + 2 * dx) % ROWS, (z + dz) % 8 * 4 + (y + dy) % 4))
                )
    return send(value, pairs)


def after(value, *others):
    return lax.optimization_barrier((value, *others))[0]


def together(*values):
    return lax.optimization_barrier(values)


def stage(value, index, cores=(0, 1), root_y=0):
    moves, at_x, at_y, at_z = (
        ([{"dy": 1}, {"dy": 3}, {"dy": 2}], (0,), (root_y,), (0,)),
        ([{"dz": 3}, {"dz": 5}], (0,), (0, 1, 2, 3), (0,)),
        ([{"dz": 1}, {"dz": 7}], (0,), (0, 1, 2, 3), (0, 3, 5)),
        ([{"dx": 1}, {"dx": 3}, {"dx": 2}], (0,), (0, 1, 2, 3), range(8)),
    )[index]
    parts = []
    for move in moves:
        zs = (0, 3) if move == {"dz": 7} else at_z

        def keep(p, s, zs=zs):
            return p // 2 in at_x and p % 2 in cores and s % 4 in at_y and s // 4 in zs

        parts.append(shifted(value, keep=keep, **move))
    return parts


def scatter_rows(own):
    parts = []
    for i in range(4):
        pairs = []
        for q in range(4):
            for t in range(8):
                row = 8 * q + t // 4 * 4
                pairs.append(((0, 8 * q + t), (t, row + i)))
                pairs.append(((1, 8 * q + t), (t, row + (i + 2) % 4)))
        parts.append(send(own[256 * i : 256 * (i + 1)], pairs))
    return parts


def halve_rows(parts):
    low, high = parts[0] + parts[1], parts[2] + parts[3]
    here = jnp.concatenate([low[:128], high[:128]], axis=0)
    there = jnp.concatenate([low[128:], high[128:]], axis=0)
    pairs = []
    for q in range(ROWS):
        for c in range(0, COLS, 8):
            for y in range(4):
                z = q // 4 * 4
                pairs.append(((q, c + z + y), (q, c + 4 - z + y)))
    return here, send(there, pairs)


def eliminate(block):
    sub = lax.broadcasted_iota(jnp.int32, (8, 128), 0)
    lane = lax.broadcasted_iota(jnp.int32, (8, 128), 1)
    full = lambda x: jnp.broadcast_to(x, (8, 128))
    left = [block[8 * i : 8 * i + 8, :] for i in range(16)]
    right = [jnp.where(lane == sub + 8 * i, 1.0, 0.0) for i in range(16)]
    upper, inverse = [], []
    for b in range(16):
        c = 8 * b
        rows = left[b]
        cols = [full(rows[:, c + k : c + k + 1]) for k in range(8)]
        e = [[full(cols[k][i : i + 1, :]) if i >= k else None for k in range(8)] for i in range(8)]
        rec = []
        low = [[None] * 8 for _ in range(8)]
        for j in range(8):
            rec.append(1.0 / e[j][j])
            for i in range(j + 1, 8):
                low[i][j] = e[i][j] * rec[j]
            for i in range(j + 1, 8):
                for k in range(j + 1, i + 1):
                    e[i][k] = e[i][k] - low[i][j] * e[k][j]
        n = [[None] * 8 for _ in range(8)]
        for j in range(8):
            for i in range(j + 1, 8):
                t = low[i][j]
                for k in range(j + 1, i):
                    t = t + low[i][k] * n[k][j]
                n[i][j] = -t
        scale = [lax.rsqrt(e[j][j]) for j in range(8)]
        s = [[None] * 8 for _ in range(8)]
        for i in range(8):
            for j in range(i + 1):
                t = rec[i] * n[i][j] if j < i else rec[i]
                for k in range(i + 1, 8):
                    t = t + (n[k][i] * rec[k]) * n[k][j]
                s[i][j] = t
                s[j][i] = t
        row_left = [full(rows[k : k + 1, :]) for k in range(8)]
        row_right = [full(right[b][k : k + 1, :]) for k in range(8)]
        def stack(parts):
            v = parts[0]
            for i in range(1, 8):
                if parts[i] is not None:
                    v = jnp.where(sub == i, parts[i], v if v is not None else 0.0)
            return v if v is not None else None
        gl = gr = ul = ur = None
        for k in range(8):
            sc = stack([s[i][k] for i in range(8)])
            col = jnp.where(sub == k, scale[k], 0.0)
            for i in range(k + 1, 8):
                col = jnp.where(sub == i, n[i][k] * scale[i], col)
            a1, a2, a3, a4 = sc * row_left[k], sc * row_right[k], col * row_left[k], col * row_right[k]
            gl = a1 if gl is None else gl + a1
            gr = a2 if gr is None else gr + a2
            ul = a3 if ul is None else ul + a3
            ur = a4 if ur is None else ur + a4
        upper.append(jnp.where(lane >= sub + c, ul, 0.0))
        inverse.append(ur)
        gl_rows = [full(gl[k : k + 1, :]) for k in range(8)]
        gr_rows = [full(gr[k : k + 1, :]) for k in range(8)]
        for i in range(b + 1, 16):
            tl = tr = None
            for k in range(8):
                f = full(left[i][:, c + k : c + k + 1])
                x, y = f * gl_rows[k], f * gr_rows[k]
                tl = x if tl is None else tl + x
                tr = y if tr is None else tr + y
            left[i] = left[i] - tl
            right[i] = right[i] - tr
    return jnp.concatenate(upper, 0), jnp.concatenate(inverse, 0)


def factor_part(work, upper, inverse):
    upper[128:256, 0:128] = jnp.zeros((128, 128), jnp.float32)
    inverse[0:128, 128:256] = jnp.zeros((128, 128), jnp.float32)

    @pl.loop(0, 2)
    def _(k):
        here = pl.ds(pl.multiple_of(128 * k, 128), 128)
        up, inv = eliminate(work[here, here])
        upper[here, here] = up
        inverse[here, here] = inv

        @pl.when(k == 0)
        def _():
            right = dot(inv, work[0:128, 128:256])
            upper[0:128, 128:256] = right
            work[128:256, 128:256] -= dot(right, right, ((0,), (0,)))

    down = dot(upper[0:128, 128:256], inverse[0:128, 0:128], ((0,), (0,)))
    inverse[128:256, 0:128] = -dot(inverse[128:256, 128:256], down)


def factor_first_kernel(mine, other, upper, inverse, work):
    for h in range(2):
        rows = pl.ds(h, 128, stride=2)
        work[0:128, 128 * h : 128 * h + 128] = mine[rows, :] + other[rows, :]
    work[128:256, 128:256] = mine[256:384, :] + other[256:384, :]
    factor_part(work, upper, inverse)


def factor_second_kernel(place, mine, other, upper0, inverse0, upper, inverse, work, up, inv):
    odd = place[0] % 2 == 1
    side = up
    for h in range(2):
        lanes = slice(128 * h, 128 * h + 128)
        here, there = mine[pl.ds(h, 256, stride=2), :], other[pl.ds(h, 256, stride=2), :]
        side[:, lanes] = jnp.where(odd, there, here)
        work[:, lanes] = jnp.where(odd, here, there)
    right = dot(inverse0[...], side[...])
    work[...] -= dot(right, right, ((0,), (0,)))
    factor_part(work, up, inv)
    zero = jnp.zeros((256, 256), jnp.float32)
    upper[0] = upper0[...]
    upper[1] = up[...]
    inverse[0:256, 0:256] = inverse0[...]
    inverse[0:256, 256:512] = zero
    inverse[256:512, 256:512] = inv[...]
    inverse[256:512, 0:256] = -dot(inv[...], dot(right, inverse0[...], ((0,), (0,))))


VMEM = pl.BlockSpec(memory_space=pltpu.VMEM)
SMEM = pl.BlockSpec(memory_space=pltpu.SMEM)


def factor_first(mine, other):
    block = jax.ShapeDtypeStruct((256, 256), jnp.float32)
    return pl.pallas_call(
        factor_first_kernel,
        out_shape=(block, block),
        in_specs=[VMEM, VMEM],
        out_specs=(VMEM, VMEM),
        scratch_shapes=[pltpu.VMEM((256, 256), jnp.float32)],
        compiler_params=pltpu.CompilerParams(vmem_limit_bytes=16 << 20),
        cost_estimate=pl.CostEstimate(flops=60_000_000_000, bytes_accessed=1 << 20, transcendentals=0),
        name="factor_first",
    )(mine, other)


def factor_second(place, mine, other, upper, inverse):
    return pl.pallas_call(
        factor_second_kernel,
        out_shape=(
            jax.ShapeDtypeStruct((2, 256, 256), jnp.float32),
            jax.ShapeDtypeStruct((512, 512), jnp.float32),
        ),
        in_specs=[SMEM, VMEM, VMEM, VMEM, VMEM],
        out_specs=(VMEM, VMEM),
        scratch_shapes=[pltpu.VMEM((256, 256), jnp.float32) for _ in range(3)],
        compiler_params=pltpu.CompilerParams(vmem_limit_bytes=16 << 20),
        cost_estimate=pl.CostEstimate(flops=60_000_000_000, bytes_accessed=1 << 20, transcendentals=0),
        name="factor_second",
    )(place, mine, other, upper, inverse)


FAR_Z = (0, 1, 7, 2, 6, 3, 5, 4)
FAR_Y = (0, 1, 3, 2)


def split(value):
    high = value.astype(jnp.bfloat16)
    return high, (value - high.astype(jnp.float32)).astype(jnp.bfloat16)


def place_part(place, g, part_of, high, low, base):
    p, s = place[0], place[1]
    zz = (s // 4 + 8 - FAR_Z[g]) % 8
    q, late = zz // 2, jnp.where(zz % 2 == p // 4, 0, 32)
    for u in range(4):
        yy = (s % 4 + 4 - FAR_Y[u]) % 4
        part, first = part_of(u)
        for slot in range(2):
            if slot == 0:
                k = jnp.where(yy < 2, 64 * yy, 128 + 64 * yy) + late
            else:
                k = jnp.where(yy < 2, 384 + 64 * yy, 64 * yy) + late
            rows = pl.ds(pl.multiple_of(base * q * 512 + k, 32), 32)
            for ch in range(4):
                lanes = slice(128 * ch, 128 * ch + 128)
                value = part[pl.ds(first + 128 * slot + ch, 32, stride=4), :]
                high[rows, lanes], low[rows, lanes] = split(value)


def gather_kernel(place, *refs):
    parts, (high, low) = refs[:7], refs[7:]
    last = (place[1] // 4 + 4) % 8 // 2
    rows = pl.ds(pl.multiple_of(last * 512, 512), 512)
    high[rows, :] = jnp.zeros((512, 512), jnp.bfloat16)
    low[rows, :] = jnp.zeros((512, 512), jnp.bfloat16)
    for g in range(7):
        place_part(place, g, lambda u, g=g: (parts[g], 256 * u), high, low, 1)


def gather(place, parts):
    wide = jax.ShapeDtypeStruct((2048, 512), jnp.bfloat16)
    return pl.pallas_call(
        gather_kernel,
        out_shape=(wide, wide),
        in_specs=[SMEM] + [VMEM] * 7,
        out_specs=(VMEM, VMEM),
        compiler_params=pltpu.CompilerParams(vmem_limit_bytes=24 << 20),
        cost_estimate=pl.CostEstimate(flops=8_000_000_000, bytes_accessed=8 << 20, transcendentals=0),
        name="gather",
    )(place, *parts)


def update_kernel(place, a, high, low, end0, end1, mine, other, upper, inverse, *refs):
    out, weight, more_high, more_low, w_both = refs
    r = pl.program_id(0)
    p, s = place[0], place[1]

    @pl.when(r == 0)
    def _():
        more_high[...] = jnp.zeros((512, 512), jnp.bfloat16)
        more_low[...] = jnp.zeros((512, 512), jnp.bfloat16)
        ends = (end0, end1)
        place_part(place, 7, lambda u: (ends[u // 2], 256 * (u % 2)), more_high, more_low, 0)
        odd = p % 2 == 1
        for ch in range(4):
            lanes = slice(128 * ch, 128 * ch + 128)
            here, there = mine[pl.ds(ch, 256, stride=4), :], other[pl.ds(ch, 256, stride=4), :]
            weight[0:256, lanes] = jnp.where(odd, there, here)
            weight[256:512, lanes] = jnp.where(odd, here, there)
        half = dot(inverse[...], weight[...])
        row = lax.broadcasted_iota(jnp.int32, (512, 512), 0)
        col = lax.broadcasted_iota(jnp.int32, (512, 512), 1)
        pick = jnp.where(row == col + 256 * s, -1.0, 0.0)
        half = jnp.where((col < 256) & (s < 2), pick, half)
        w_both[:, 0:512], w_both[:, 512:1024] = split(dot(inverse[...], half, ((0,), (0,))))

    c, q = r // 4, r % 4
    lanes = pl.ds(pl.multiple_of(c * 256, 256), 256)
    block = (pl.ds(pl.multiple_of(q * 512, 512), 512), lanes)
    last = q == (s // 4 + 4) % 8 // 2
    zero = jnp.zeros((512, 256), jnp.bfloat16)
    x_high = high[block] + jnp.where(last, more_high[:, lanes], zero)
    x_low = low[block] + jnp.where(last, more_low[:, lanes], zero)

    def times(x, w):
        return lax.dot_general(x, w, (((0,), (0,)), ((), ())), preferred_element_type=jnp.float32)

    both = times(x_high, w_both[...])
    product = both[:, 0:512] + (both[:, 512:1024] + times(x_low, w_both[:, 0:512]))
    for ch in range(4):
        kept = a[pl.ds(ch, 256, stride=4), :]
        if ch < 2:
            kept = jnp.where(s < 2, 0.0, kept)
        out[pl.ds(ch, 256, stride=4), :] = kept - product[:, 128 * ch : 128 * ch + 128]

    @pl.when((r == 0) & (p < 2))
    def _():
        for ch in range(4):
            where = pl.ds(ch, 256, stride=4)
            if ch >= 2:
                out[where, :] = jnp.zeros((256, 128), jnp.float32)
            else:
                diagonal = upper[jnp.minimum(p, 1), 128 * ch : 128 * ch + 128, :].T
                natural = out[where, :]
                out[where, :] = jnp.where(s == p, diagonal, jnp.where(s > p, 0.0, natural))


def update(place, a, high, low, ends, mine, other, upper, inverse):
    return pl.pallas_call(
        update_kernel,
        out_shape=jax.ShapeDtypeStruct(a.shape, jnp.float32),
        grid=(8,),
        in_specs=[SMEM, pl.BlockSpec((1024, 128), lambda r: (r, 0))] + [VMEM] * 8,
        out_specs=pl.BlockSpec((1024, 128), lambda r: (r, 0)),
        scratch_shapes=[
            pltpu.VMEM((512, 512), jnp.float32),
            pltpu.VMEM((512, 512), jnp.bfloat16),
            pltpu.VMEM((512, 512), jnp.bfloat16),
            pltpu.VMEM((512, 1024), jnp.bfloat16),
        ],
        compiler_params=pltpu.CompilerParams(vmem_limit_bytes=40 << 20),
        cost_estimate=pl.CostEstimate(flops=8_000_000_000, bytes_accessed=16 << 20, transcendentals=0),
        name="update",
    )(place, a, high, low, *ends, mine, other, upper, inverse)


def per_device(kernel):
    p, s = lax.axis_index("prow"), lax.axis_index("pcol")
    place = jnp.stack([p, s]).astype(jnp.int32)
    a = kernel.reshape(8192, 128)
    own = a[:1024]
    block = own.reshape(256, 4, 128)[:, :2]

    rows = scatter_rows(own)

    first = jnp.concatenate([block[:128].reshape(256, 128), block[128:, 1]], axis=0)
    first = jnp.where((p == 0) & (s == 0), first, sum(stage(first, 0, (0,))))
    second = together(block.reshape(512, 128), first)[0]
    second = jnp.where((p < 2) & (s == 1), second, sum(stage(second, 0, (0, 1), 1)))
    first = first + sum(stage(first, 1, (0,)))
    first = first + sum(stage(first, 2, (0,)))
    here, moved = halve_rows(rows)
    near = jnp.where(p // 4 == s // 4 % 2, here, moved)
    near = together(near, first)[0]
    column = [near] + [shifted(near, dy=k) for k in (1, 3, 2)]
    column = jnp.concatenate(column, axis=0)
    second = second + sum(stage(second, 1))
    parts = stage(first, 3, (0,))
    column, second, first = together(column, second, first)

    up1, down1 = shifted(column, dz=1), shifted(column, dz=7)
    first = first + sum(parts)
    first_other = send(first, [((q, c), (q + 1, c)) for q in range(0, ROWS, 2) for c in range(COLS)])
    parts = stage(second, 2)
    up1, down1, first, first_other, second, *parts = together(
        up1, down1, first, first_other, second, *parts
    )

    second = second + sum(parts)
    parts = stage(second, 3)
    up2, down2 = shifted(up1, dz=1), shifted(down1, dz=7)
    upper, inverse = factor_first(first, first_other)
    up2, down2, second, upper, inverse, *parts = together(
        up2, down2, second, upper, inverse, *parts
    )

    second = second + sum(parts)
    second_other = swap_cores(second)
    mine = stage(together(own, upper)[0], 3)
    up3, down3 = shifted(up2, dz=1), shifted(down2, dz=7)
    upper, inverse = factor_second(place, second, second_other, upper, inverse)
    up3, down3, upper, inverse = together(up3, down3, upper, inverse)

    up4, down4 = shifted(up3[:512], dz=1), shifted(down3[512:], dz=7)
    high, low = gather(place, [column, up1, down1, up2, down2, up3, down3])
    up4, down4, high, low, *mine = together(up4, down4, high, low, *mine)
    mine = jnp.where(p < 2, own, sum(mine))
    other = swap_cores(mine)
    out = update(place, a, high, low, (up4, down4), mine, other, upper, inverse)
    return out.reshape(kernel.shape)


def solution(mesh):
    spec = P(None, "prow", None, None, "pcol", None)
    return jax.shard_map(per_device, mesh=mesh, in_specs=(spec,), out_specs=spec, check_vma=False)
```

```python
import jax
import jax.numpy as jnp
from jax import lax
from jax.experimental import pallas as pl
from jax.experimental.pallas import tpu as pltpu
from jax.sharding import PartitionSpec as P

AXES = ("prow", "pcol")
ROWS, COLS = 8, 32
HIGHEST = lax.Precision.HIGHEST


def dot(a, b, dims=((1,), (0,))):
    return lax.dot_general(
        a, b, (dims, ((), ())), precision=HIGHEST, preferred_element_type=jnp.float32
    )


def send(value, pairs):
    flat = [(p * COLS + s, u * COLS + v) for (p, s), (u, v) in pairs]
    return lax.ppermute(value, AXES, flat)


def swap_cores(value):
    return send(value, [((p, s), (p ^ 1, s)) for p in range(ROWS) for s in range(COLS)])


def shifted(value, dx=0, dy=0, dz=0, keep=lambda p, s: True):
    pairs = []
    for p in range(ROWS):
        for s in range(COLS):
            if keep(p, s):
                z, y = divmod(s, 4)
                pairs.append(
                    ((p, s), ((p + 2 * dx) % ROWS, (z + dz) % 8 * 4 + (y + dy) % 4))
                )
    return send(value, pairs)


def after(value, *others):
    return lax.optimization_barrier((value, *others))[0]


def together(*values):
    return lax.optimization_barrier(values)


def stage(value, index, cores=(0, 1), root_y=0):
    moves, at_x, at_y, at_z = (
        ([{"dy": 1}, {"dy": 3}, {"dy": 2}], (0,), (root_y,), (0,)),
        ([{"dz": 3}, {"dz": 5}], (0,), (0, 1, 2, 3), (0,)),
        ([{"dz": 1}, {"dz": 7}], (0,), (0, 1, 2, 3), (0, 3, 5)),
        ([{"dx": 1}, {"dx": 3}, {"dx": 2}], (0,), (0, 1, 2, 3), range(8)),
    )[index]
    parts = []
    for move in moves:
        zs = (0, 3) if move == {"dz": 7} else at_z

        def keep(p, s, zs=zs):
            return p // 2 in at_x and p % 2 in cores and s % 4 in at_y and s // 4 in zs

        parts.append(shifted(value, keep=keep, **move))
    return parts


def scatter_rows(own):
    parts = []
    for i in range(4):
        pairs = []
        for q in range(4):
            for t in range(8):
                row = 8 * q + t // 4 * 4
                pairs.append(((0, 8 * q + t), (t, row + i)))
                pairs.append(((1, 8 * q + t), (t, row + (i + 2) % 4)))
        parts.append(send(own[256 * i : 256 * (i + 1)], pairs))
    return parts


def halve_rows(parts):
    low, high = parts[0] + parts[1], parts[2] + parts[3]
    here = jnp.concatenate([low[:128], high[:128]], axis=0)
    there = jnp.concatenate([low[128:], high[128:]], axis=0)
    pairs = []
    for q in range(ROWS):
        for c in range(0, COLS, 8):
            for y in range(4):
                z = q // 4 * 4
                pairs.append(((q, c + z + y), (q, c + 4 - z + y)))
    return here, send(there, pairs)


def eliminate(block):
    sub = lax.broadcasted_iota(jnp.int32, (8, 128), 0)
    lane = lax.broadcasted_iota(jnp.int32, (8, 128), 1)
    full = lambda x: jnp.broadcast_to(x, (8, 128))
    left = [block[8 * i : 8 * i + 8, :] for i in range(16)]
    right = [jnp.where(lane == sub + 8 * i, 1.0, 0.0) for i in range(16)]
    upper, inverse = [], []
    for b in range(16):
        c = 8 * b
        rows = left[b]
        cols = [full(rows[:, c + k : c + k + 1]) for k in range(8)]
        e = [[full(cols[k][i : i + 1, :]) if i >= k else None for k in range(8)] for i in range(8)]
        rec = []
        low = [[None] * 8 for _ in range(8)]
        for j in range(8):
            rec.append(1.0 / e[j][j])
            for i in range(j + 1, 8):
                low[i][j] = e[i][j] * rec[j]
            for i in range(j + 1, 8):
                for k in range(j + 1, i + 1):
                    e[i][k] = e[i][k] - low[i][j] * e[k][j]
        n = [[None] * 8 for _ in range(8)]
        for j in range(8):
            for i in range(j + 1, 8):
                t = low[i][j]
                for k in range(j + 1, i):
                    t = t + low[i][k] * n[k][j]
                n[i][j] = -t
        scale = [lax.rsqrt(e[j][j]) for j in range(8)]
        s = [[None] * 8 for _ in range(8)]
        for i in range(8):
            for j in range(i + 1):
                t = rec[i] * n[i][j] if j < i else rec[i]
                for k in range(i + 1, 8):
                    t = t + (n[k][i] * rec[k]) * n[k][j]
                s[i][j] = t
                s[j][i] = t
        row_left = [full(rows[k : k + 1, :]) for k in range(8)]
        row_right = [full(right[b][k : k + 1, :]) for k in range(8)]
        def stack(parts):
            v = parts[0]
            for i in range(1, 8):
                if parts[i] is not None:
                    v = jnp.where(sub == i, parts[i], v if v is not None else 0.0)
            return v if v is not None else None
        gl = gr = ul = ur = None
        for k in range(8):
            sc = stack([s[i][k] for i in range(8)])
            col = jnp.where(sub == k, scale[k], 0.0)
            for i in range(k + 1, 8):
                col = jnp.where(sub == i, n[i][k] * scale[i], col)
            a1, a2, a3, a4 = sc * row_left[k], sc * row_right[k], col * row_left[k], col * row_right[k]
            gl = a1 if gl is None else gl + a1
            gr = a2 if gr is None else gr + a2
            ul = a3 if ul is None else ul + a3
            ur = a4 if ur is None else ur + a4
        upper.append(jnp.where(lane >= sub + c, ul, 0.0))
        inverse.append(ur)
        gl_rows = [full(gl[k : k + 1, :]) for k in range(8)]
        gr_rows = [full(gr[k : k + 1, :]) for k in range(8)]
        for i in range(b + 1, 16):
            tl = tr = None
            for k in range(8):
                f = full(left[i][:, c + k : c + k + 1])
                x, y = f * gl_rows[k], f * gr_rows[k]
                tl = x if tl is None else tl + x
                tr = y if tr is None else tr + y
            left[i] = left[i] - tl
            right[i] = right[i] - tr
    return jnp.concatenate(upper, 0), jnp.concatenate(inverse, 0)


def factor_part(work, upper, inverse):
    upper[128:256, 0:128] = jnp.zeros((128, 128), jnp.float32)
    inverse[0:128, 128:256] = jnp.zeros((128, 128), jnp.float32)

    @pl.loop(0, 2)
    def _(k):
        here = pl.ds(pl.multiple_of(128 * k, 128), 128)
        up, inv = eliminate(work[here, here])
        upper[here, here] = up
        inverse[here, here] = inv

        @pl.when(k == 0)
        def _():
            right = dot(inv, work[0:128, 128:256])
            upper[0:128, 128:256] = right
            work[128:256, 128:256] -= dot(right, right, ((0,), (0,)))

    down = dot(upper[0:128, 128:256], inverse[0:128, 0:128], ((0,), (0,)))
    inverse[128:256, 0:128] = -dot(inverse[128:256, 128:256], down)


def factor_first_kernel(mine, other, upper, inverse, work):
    for h in range(2):
        rows = pl.ds(h, 128, stride=2)
        work[0:128, 128 * h : 128 * h + 128] = mine[rows, :] + other[rows, :]
    work[128:256, 128:256] = mine[256:384, :] + other[256:384, :]
    factor_part(work, upper, inverse)


def factor_second_kernel(place, mine, other, upper0, inverse0, upper, inverse, work, up, inv):
    odd = place[0] % 2 == 1
    side = up
    for h in range(2):
        lanes = slice(128 * h, 128 * h + 128)
        here, there = mine[pl.ds(h, 256, stride=2), :], other[pl.ds(h, 256, stride=2), :]
        side[:, lanes] = jnp.where(odd, there, here)
        work[:, lanes] = jnp.where(odd, here, there)
    right = dot(inverse0[...], side[...])
    work[...] -= dot(right, right, ((0,), (0,)))
    factor_part(work, up, inv)
    zero = jnp.zeros((256, 256), jnp.float32)
    upper[0] = upper0[...]
    upper[1] = up[...]
    inverse[0:256, 0:256] = inverse0[...]
    inverse[0:256, 256:512] = zero
    inverse[256:512, 256:512] = inv[...]
    inverse[256:512, 0:256] = -dot(inv[...], dot(right, inverse0[...], ((0,), (0,))))


VMEM = pl.BlockSpec(memory_space=pltpu.VMEM)
SMEM = pl.BlockSpec(memory_space=pltpu.SMEM)


def factor_first(mine, other):
    block = jax.ShapeDtypeStruct((256, 256), jnp.float32)
    return pl.pallas_call(
        factor_first_kernel,
        out_shape=(block, block),
        in_specs=[VMEM, VMEM],
        out_specs=(VMEM, VMEM),
        scratch_shapes=[pltpu.VMEM((256, 256), jnp.float32)],
        compiler_params=pltpu.CompilerParams(vmem_limit_bytes=16 << 20),
        cost_estimate=pl.CostEstimate(flops=60_000_000_000, bytes_accessed=1 << 20, transcendentals=0),
        name="factor_first",
    )(mine, other)


def factor_second(place, mine, other, upper, inverse):
    return pl.pallas_call(
        factor_second_kernel,
        out_shape=(
            jax.ShapeDtypeStruct((2, 256, 256), jnp.float32),
            jax.ShapeDtypeStruct((512, 512), jnp.float32),
        ),
        in_specs=[SMEM, VMEM, VMEM, VMEM, VMEM],
        out_specs=(VMEM, VMEM),
        scratch_shapes=[pltpu.VMEM((256, 256), jnp.float32) for _ in range(3)],
        compiler_params=pltpu.CompilerParams(vmem_limit_bytes=16 << 20),
        cost_estimate=pl.CostEstimate(flops=60_000_000_000, bytes_accessed=1 << 20, transcendentals=0),
        name="factor_second",
    )(place, mine, other, upper, inverse)


FAR_Z = (0, 1, 7, 2, 6, 3, 5, 4)
FAR_Y = (0, 1, 3, 2)


def split(value):
    high = value.astype(jnp.bfloat16)
    return high, (value - high.astype(jnp.float32)).astype(jnp.bfloat16)


def place_part(place, g, part_of, high, low, base):
    p, s = place[0], place[1]
    zz = (s // 4 + 8 - FAR_Z[g]) % 8
    q, late = zz // 2, jnp.where(zz % 2 == p // 4, 0, 32)
    for u in range(4):
        yy = (s % 4 + 4 - FAR_Y[u]) % 4
        part, first = part_of(u)
        for slot in range(2):
            if slot == 0:
                k = jnp.where(yy < 2, 64 * yy, 128 + 64 * yy) + late
            else:
                k = jnp.where(yy < 2, 384 + 64 * yy, 64 * yy) + late
            rows = pl.ds(pl.multiple_of(base * q * 512 + k, 32), 32)
            for ch in range(4):
                lanes = slice(128 * ch, 128 * ch + 128)
                value = part[pl.ds(first + 128 * slot + ch, 32, stride=4), :]
                high[rows, lanes], low[rows, lanes] = split(value)


def gather_kernel(place, *refs):
    parts, (high, low) = refs[:7], refs[7:]
    last = (place[1] // 4 + 4) % 8 // 2
    rows = pl.ds(pl.multiple_of(last * 512, 512), 512)
    high[rows, :] = jnp.zeros((512, 512), jnp.bfloat16)
    low[rows, :] = jnp.zeros((512, 512), jnp.bfloat16)
    for g in range(7):
        place_part(place, g, lambda u, g=g: (parts[g], 256 * u), high, low, 1)


def gather(place, parts):
    wide = jax.ShapeDtypeStruct((2048, 512), jnp.bfloat16)
    return pl.pallas_call(
        gather_kernel,
        out_shape=(wide, wide),
        in_specs=[SMEM] + [VMEM] * 7,
        out_specs=(VMEM, VMEM),
        compiler_params=pltpu.CompilerParams(vmem_limit_bytes=24 << 20),
        cost_estimate=pl.CostEstimate(flops=8_000_000_000, bytes_accessed=8 << 20, transcendentals=0),
        name="gather",
    )(place, *parts)


def update_kernel(place, a, high, low, end0, end1, mine, other, upper, inverse, *refs):
    out, weight, more_high, more_low, w_both = refs
    r = pl.program_id(0)
    p, s = place[0], place[1]

    @pl.when(r == 0)
    def _():
        more_high[...] = jnp.zeros((512, 512), jnp.bfloat16)
        more_low[...] = jnp.zeros((512, 512), jnp.bfloat16)
        ends = (end0, end1)
        place_part(place, 7, lambda u: (ends[u // 2], 256 * (u % 2)), more_high, more_low, 0)
        odd = p % 2 == 1
        for ch in range(4):
            lanes = slice(128 * ch, 128 * ch + 128)
            here, there = mine[pl.ds(ch, 256, stride=4), :], other[pl.ds(ch, 256, stride=4), :]
            weight[0:256, lanes] = jnp.where(odd, there, here)
            weight[256:512, lanes] = jnp.where(odd, here, there)
        half = dot(inverse[...], weight[...])
        row = lax.broadcasted_iota(jnp.int32, (512, 512), 0)
        col = lax.broadcasted_iota(jnp.int32, (512, 512), 1)
        pick = jnp.where(row == col + 256 * s, -1.0, 0.0)
        half = jnp.where((col < 256) & (s < 2), pick, half)
        w_both[:, 0:512], w_both[:, 512:1024] = split(dot(inverse[...], half, ((0,), (0,))))

    c, q = r // 4, r % 4
    lanes = pl.ds(pl.multiple_of(c * 256, 256), 256)
    block = (pl.ds(pl.multiple_of(q * 512, 512), 512), lanes)
    last = q == (s // 4 + 4) % 8 // 2
    zero = jnp.zeros((512, 256), jnp.bfloat16)
    x_high = high[block] + jnp.where(last, more_high[:, lanes], zero)
    x_low = low[block] + jnp.where(last, more_low[:, lanes], zero)

    def times(x, w):
        return lax.dot_general(x, w, (((0,), (0,)), ((), ())), preferred_element_type=jnp.float32)

    both = times(x_high, w_both[...])
    product = both[:, 0:512] + (both[:, 512:1024] + times(x_low, w_both[:, 0:512]))
    for ch in range(4):
        kept = a[pl.ds(ch, 256, stride=4), :]
        if ch < 2:
            kept = jnp.where(s < 2, 0.0, kept)
        out[pl.ds(ch, 256, stride=4), :] = kept - product[:, 128 * ch : 128 * ch + 128]

    @pl.when((r == 0) & (p < 2))
    def _():
        for ch in range(4):
            where = pl.ds(ch, 256, stride=4)
            if ch >= 2:
                out[where, :] = jnp.zeros((256, 128), jnp.float32)
            else:
                diagonal = upper[jnp.minimum(p, 1), 128 * ch : 128 * ch + 128, :].T
                natural = out[where, :]
                out[where, :] = jnp.where(s == p, diagonal, jnp.where(s > p, 0.0, natural))


def update(place, a, high, low, ends, mine, other, upper, inverse):
    return pl.pallas_call(
        update_kernel,
        out_shape=jax.ShapeDtypeStruct(a.shape, jnp.float32),
        grid=(8,),
        in_specs=[SMEM, pl.BlockSpec((1024, 128), lambda r: (r, 0))] + [VMEM] * 8,
        out_specs=pl.BlockSpec((1024, 128), lambda r: (r, 0)),
        scratch_shapes=[
            pltpu.VMEM((512, 512), jnp.float32),
            pltpu.VMEM((512, 512), jnp.bfloat16),
            pltpu.VMEM((512, 512), jnp.bfloat16),
            pltpu.VMEM((512, 1024), jnp.bfloat16),
        ],
        compiler_params=pltpu.CompilerParams(vmem_limit_bytes=40 << 20),
        cost_estimate=pl.CostEstimate(flops=8_000_000_000, bytes_accessed=16 << 20, transcendentals=0),
        name="update",
    )(place, a, high, low, *ends, mine, other, upper, inverse)


def per_device(kernel):
    p, s = lax.axis_index("prow"), lax.axis_index("pcol")
    place = jnp.stack([p, s]).astype(jnp.int32)
    a = kernel.reshape(8192, 128)
    own = a[:1024]
    block = own.reshape(256, 4, 128)[:, :2]

    rows = scatter_rows(own)

    first = jnp.concatenate([block[:128].reshape(256, 128), block[128:, 1]], axis=0)
    first = jnp.where((p == 0) & (s == 0), first, sum(stage(first, 0, (0,))))
    second = together(block.reshape(512, 128), first)[0]
    second = jnp.where((p < 2) & (s == 1), second, sum(stage(second, 0, (0, 1), 1)))
    first = first + sum(stage(first, 1, (0,)))
    first = first + sum(stage(first, 2, (0,)))
    here, moved = halve_rows(rows)
    near = jnp.where(p // 4 == s // 4 % 2, here, moved)
    near = together(near, first)[0]
    column = [near] + [shifted(near, dy=k) for k in (1, 3, 2)]
    column = jnp.concatenate(column, axis=0)
    second = second + sum(stage(second, 1))
    parts = stage(first, 3, (0,))
    column, second, first = together(column, second, first)

    up1, down1 = shifted(column, dz=1), shifted(column, dz=7)
    first = first + sum(parts)
    first_other = send(first, [((q, c), (q + 1, c)) for q in range(0, ROWS, 2) for c in range(COLS)])
    parts = stage(second, 2)
    up1, down1, first, first_other, second, *parts = together(
        up1, down1, first, first_other, second, *parts
    )

    second = second + sum(parts)
    parts = stage(second, 3)
    up2, down2 = shifted(up1, dz=1), shifted(down1, dz=7)
    upper, inverse = factor_first(first, first_other)
    up2, down2, second, upper, inverse, *parts = together(
        up2, down2, second, upper, inverse, *parts
    )

    second = second + sum(parts)
    second_other = swap_cores(second)
    mine = stage(together(own, upper)[0], 3)
    up3, down3 = shifted(up2, dz=1), shifted(down2, dz=7)
    upper, inverse = factor_second(place, second, second_other, upper, inverse)
    up3, down3, upper, inverse = together(up3, down3, upper, inverse)

    up4, down4 = shifted(up3[:512], dz=1), shifted(down3[512:], dz=7)
    high, low = gather(place, [column, up1, down1, up2, down2, up3, down3])
    up4, down4, high, low = together(up4, down4, high, low)
    mine = jnp.where(p < 2, own, sum(mine))
    other = swap_cores(mine)
    out = update(place, a, high, low, (up4, down4), mine, other, upper, inverse)
    return out.reshape(kernel.shape)


def solution(mesh):
    spec = P(None, "prow", None, None, "pcol", None)
    return jax.shard_map(per_device, mesh=mesh, in_specs=(spec,), out_specs=spec, check_vma=False)
```
